256 devices in a mesh: tm: 32 (over y, x, core), rows: 8 (over z).
Axes of the slice: x: 4, y: 4, z: 8, core: 2. Of those that a mesh axis runs over, the one named last changes fastest.
Arguments:
- features: bfloat16 [128, 64, 32, 512], P('tm', 'rows'), may hold values from -80 to 80
- gain_in: float32 [512], replicated, may hold values from 0.5 to 2
- shift_in: float32 [512], replicated, may hold values from -3 to 3
- conv_in: bfloat16 [3, 3, 3, 512, 256], replicated, may hold values from -0.0546875 to 0.0546875
- gain_mid: float32 [256], replicated, may hold values from 0.5 to 2
- shift_mid: float32 [256], replicated, may hold values from -3 to 3
- conv_out: bfloat16 [3, 3, 3, 256, 256], replicated, may hold values from -0.078125 to 0.078125
- shortcut: bfloat16 [512, 256], replicated, may hold values from -0.25 to 0.25
Outputs:
- decoded: bfloat16 [128, 64, 32, 256], P('tm', 'rows')
The draws below stay inside these ranges and needn't reach their ends.
All inputs are finite; a program needn't handle non-finite values.
Results may differ from the reference program's by a relative error of at most 0.012.
Values may be sent and summed in bfloat16 or wider, within the bound.
A program may use at most 128 MiB of HBM per device.

```python
import math
import jax
import jax.numpy as jnp
from jax import lax

C_IN = 512
C_OUT = 256
GROUPS = 32
FRAMES = 4
ROWS_DEV = 8
COLS = 32
TOTAL_FRAMES = 128
TOTAL_ROWS = 64


def draw_features(key, part):
    key = jax.random.fold_in(key, 11)
    first_key, second_key, third_key, fourth_key, fifth_key = jax.random.split(key, 5)
    frame_place = jnp.arange(TOTAL_FRAMES, dtype=jnp.float32) / max(TOTAL_FRAMES - 1, 1)
    row_place = jnp.arange(TOTAL_ROWS, dtype=jnp.float32) / max(TOTAL_ROWS - 1, 1)
    channel_scale = jnp.exp(math.log(10.0) * jax.random.uniform(second_key, (C_IN,), jnp.float32)) / 4.5
    offset = jax.random.uniform(third_key, (C_IN,), jnp.float32, 0.5, 1.5)
    frame_blocks = TOTAL_FRAMES // FRAMES
    row_slabs = TOTAL_ROWS // ROWS_DEV
    slab_log = jax.random.uniform(fourth_key, (row_slabs,), jnp.float32, -0.7, 0.7)
    cell_log = jax.random.uniform(fifth_key, (frame_blocks, row_slabs), jnp.float32, -0.4, 0.4)
    patch = jnp.repeat(jnp.repeat(cell_log + slab_log[None, :], FRAMES, axis=0), ROWS_DEV, axis=1)
    profile = jnp.log(1.0 + 0.5 * jnp.sin(3.0 * math.pi * row_place))
    shape = (TOTAL_FRAMES, TOTAL_ROWS, COLS, C_IN)
    frame_rate = 0.4
    lift = 1.2
    noise = jnp.clip(jax.random.normal(first_key, shape, jnp.float32), -4.0, 4.0)
    exponent = frame_rate * frame_place[:, None] + frame_place[:, None] * row_place[None, :] + profile[None, :] + patch - lift
    level = jnp.exp(exponent)
    values = (noise + offset) * level[:, :, None, None] * channel_scale
    return values.astype(jnp.bfloat16)


def scatter_about(stream_key, extent, scale, most, kind=jnp.bfloat16):
    return jnp.clip(scale * jax.random.normal(stream_key, extent, jnp.float32), -most, most).astype(kind)


def setup_inputs(seed: int = 0) -> dict:
    seeds = jax.random.split(jax.random.key(seed), 9)
    features = draw_features(jax.random.fold_in(seeds[8], 71), 0)
    gain_in = jnp.clip(jnp.exp(jax.random.uniform(seeds[1], (C_IN,), jnp.float32, math.log(0.5), math.log(2.0))), 0.5, 2.0)
    shift_in = scatter_about(seeds[2], (C_IN,), 0.5, 3.0, jnp.float32)
    conv_in = scatter_about(seeds[3], (3, 3, 3, C_IN, C_OUT), (27 * C_IN) ** -0.5, 0.0546875)
    gain_mid = jnp.clip(jnp.exp(jax.random.uniform(seeds[4], (C_OUT,), jnp.float32, math.log(0.5), math.log(2.0))), 0.5, 2.0)
    shift_mid = scatter_about(seeds[5], (C_OUT,), 0.5, 3.0, jnp.float32)
    conv_out = scatter_about(seeds[6], (3, 3, 3, C_OUT, C_OUT), (27 * C_OUT) ** -0.5, 0.078125)
    shortcut = scatter_about(seeds[7], (C_IN, C_OUT), C_IN ** -0.5, 0.25)
    return dict(features=features, gain_in=gain_in, shift_in=shift_in, conv_in=conv_in, gain_mid=gain_mid, shift_mid=shift_mid, conv_out=conv_out, shortcut=shortcut)


epsilon = 1e-06

def conv_block(extended, kernel):
    out_frames = extended.shape[0] - 2
    out_rows = extended.shape[1] - 2
    out_cols = extended.shape[2] - 2
    channels = extended.shape[3]
    width_out = kernel.shape[4]
    summed = jnp.zeros((out_frames * out_rows * out_cols, width_out), jnp.float32)
    for offset_time in range(3):
        for offset_row in range(3):
            stacked = jnp.concatenate([extended[offset_time:offset_time + out_frames, offset_row:offset_row + out_rows, offset_col:offset_col + out_cols, :] for offset_col in range(3)], axis=-1)
            matrix = kernel[offset_time, offset_row].reshape(3 * channels, width_out)
            summed = summed + jnp.dot(stacked.reshape(-1, 3 * channels), matrix, preferred_element_type=jnp.float32)
    return summed.reshape(out_frames, out_rows, out_cols, width_out)

def conv_clip(values, kernel):
    timed = jnp.concatenate([values[:1], values[:1], values], axis=0)
    padded = jnp.pad(timed, ((0, 0), (1, 1), (1, 1), (0, 0)))
    blocks = TOTAL_FRAMES // FRAMES

    def one_block(index):
        window = lax.dynamic_slice_in_dim(padded, (index * FRAMES).astype(jnp.int32), FRAMES + 2, 0)
        return conv_block(window, kernel)
    result = lax.map(one_block, jnp.arange(blocks, dtype=jnp.int32))
    return result.reshape(TOTAL_FRAMES, TOTAL_ROWS, COLS, kernel.shape[4])

def moments(values):
    shaped = values.astype(jnp.float32).reshape(values.shape[:-1] + (GROUPS, values.shape[-1] // GROUPS))
    group_mean = lax.optimization_barrier(jnp.mean(shaped, axis=(0, 1, 2, 4)))
    group_var = lax.optimization_barrier(jnp.mean(jnp.square(shaped - group_mean[:, None]), axis=(0, 1, 2, 4)))
    return (group_mean, group_var)

def activate(values, group_mean, group_var, gain, shift):
    shaped = values.astype(jnp.float32).reshape(values.shape[:-1] + (GROUPS, values.shape[-1] // GROUPS))
    normed = (shaped - group_mean[:, None]) * lax.rsqrt(group_var[:, None] + epsilon)
    normed = normed.reshape(values.shape) * gain + shift
    return jax.nn.silu(normed).astype(jnp.bfloat16)

def reference(features, gain_in, shift_in, conv_in, gain_mid, shift_mid, conv_out, shortcut):
    mean_in, var_in = moments(features)
    first = activate(features, mean_in, var_in, gain_in, shift_in)
    hidden = conv_clip(first, conv_in).astype(jnp.bfloat16)
    mean_mid, var_mid = moments(hidden)
    second = activate(hidden, mean_mid, var_mid, gain_mid, shift_mid)
    branch = conv_clip(second, conv_out)
    skipped = jnp.dot(features.reshape(-1, C_IN), shortcut, preferred_element_type=jnp.float32).reshape(branch.shape)
    return (branch + skipped).astype(jnp.bfloat16)
```

```python
import itertools

import jax
import jax.numpy as jnp
from jax import lax
from jax.experimental import pallas as pl
from jax.experimental.pallas import tpu as pltpu
from jax.sharding import PartitionSpec as P

GROUPS = 32
FRAMES = 4
ROWS = 8
COLS = 32
CELLS = FRAMES * ROWS * COLS
EPSILON = 1e-06
F32 = jnp.float32
BF16 = jnp.bfloat16
MESH = pl.DeviceIdType.MESH
SIZES = {"y": 4, "x": 4, "core": 2, "z": 8}
STAGES = (("z", "core"), ("y", "x"))
HOPS = {2: (0, 1), 4: (0, 1, 2, 1), 8: (0, 1, 2, 3, 4, 3, 2, 1)}


def offsets(axes):
    every = itertools.product(*[range(SIZES[a]) for a in axes])
    moved = [o for o in every if any(o)]
    return sorted(moved, key=lambda o: -sum(HOPS[SIZES[a]][i] for a, i in zip(axes, o)))


def group_sum(values, width):
    lane = lax.broadcasted_iota(jnp.int32, values.shape, 1)
    step = 1
    while step < width:
        up = pltpu.roll(values, 128 - step, 1)
        down = pltpu.roll(values, step, 1)
        values = values + jnp.where((lane // step) % 2 == 0, up, down)
        step *= 2
    return values


def to_rows(values):
    return jnp.concatenate([values[:, i : i + 128] for i in range(0, values.shape[1], 128)], axis=0)


def to_lanes(values):
    return jnp.concatenate([values[i : i + 1, :] for i in range(values.shape[0])], axis=1)


def local_statistics(ext):
    channels = ext.shape[-1]
    width = channels // GROUPS
    rows = channels // 128

    def slab(i):
        return ext[2 + i // ROWS, 1 + i % ROWS].astype(F32)

    def add_up(i, total):
        return total + slab(i).reshape(COLS // 8, 8, channels).sum(0)

    zero = jnp.zeros((8, channels), F32)
    total = lax.fori_loop(0, FRAMES * ROWS, add_up, zero, unroll=4).sum(0, keepdims=True)
    mean = group_sum(to_rows(total), width) * (1.0 / (CELLS * width))
    wide_mean = to_lanes(mean)

    def add_square(i, total):
        return total + jnp.square(slab(i) - wide_mean).reshape(COLS // 8, 8, channels).sum(0)

    spread = lax.fori_loop(0, FRAMES * ROWS, add_square, zero, unroll=4).sum(0, keepdims=True)
    spread = group_sum(to_rows(spread), width)
    lane = lax.broadcasted_iota(jnp.int32, (1, 128), 1)
    packed = jnp.zeros((1, 128), F32)
    for r in range(rows):
        both = jnp.where(lane % 4 < 2, mean[r : r + 1], spread[r : r + 1])
        packed = packed + jnp.where((lane % width) // 4 == r, both, 0.0)
    return packed


def combined(own, others, count):
    members = others.shape[0] + 1
    lane = lax.broadcasted_iota(jnp.int32, (1, 128), 1)
    total = own + jnp.sum(others, axis=0)
    mean = total * (1.0 / members)
    deviation = jnp.square(own - mean) + jnp.sum(jnp.square(others - mean[None]), axis=0)
    moved = pltpu.roll(deviation, 2, 1)
    return jnp.where(lane % 4 < 2, mean, total + moved * float(count))


def unpacked(packed, channels):
    width = channels // GROUPS
    rows = channels // 128
    shape = (2 * rows, 128)
    lane = lax.broadcasted_iota(jnp.int32, shape, 1)
    row = lax.broadcasted_iota(jnp.int32, shape, 0)
    wanted = jnp.where(row < rows, 4 * row, 4 * (row - rows) + 2)
    picked = jnp.where(lane % width == wanted, jnp.broadcast_to(packed, shape), 0.0)
    spread = group_sum(picked, width)
    return spread[:rows], spread[rows:]


def activate_slab(raw, out, frame, row, mean, scale, shift):
    v = (raw[frame, row].astype(F32) - mean) * scale + shift
    out[frame, row] = (v + v * jnp.tanh(v)).astype(BF16)


def convolve(act, weights, acc, first_frame, frames):
    channels = act.shape[-1]
    cells = frames * ROWS * COLS

    def one_column_tap(e, carry):
        taps = [
            act[first_frame + a : first_frame + a + frames, b : b + ROWS].reshape(cells, channels)
            for a in range(3)
            for b in range(3)
        ]
        matrix = weights[:, :, e].reshape(9 * channels, weights.shape[-1])
        acc[e, 0:cells] = jnp.dot(
            jnp.concatenate(taps, axis=-1), matrix, preferred_element_type=F32
        )
        return carry

    lax.fori_loop(0, 3, one_column_tap, 0)
    left, middle, right = acc[0, 0:cells], acc[1, 0:cells], acc[2, 0:cells]
    col = lax.broadcasted_iota(jnp.int32, left.shape, 0) % COLS
    from_left = jnp.where(col == 0, 0.0, pltpu.roll(left, 1, 0))
    from_right = jnp.where(col == COLS - 1, 0.0, pltpu.roll(right, cells - 1, 0))
    return middle + from_left + from_right


def kernel(
    x_hbm, gain_in_hbm, shift_in_hbm, w1_hbm, gain_mid_hbm, shift_mid_hbm, w2_hbm, short_hbm,
    out_ref,
    xr, xa, hr, ha, w1, w2, short, acc, skip, gain_in, shift_in, gain_mid, shift_mid,
    stat_out, stat_in_a, stat_in_b,
    load_sem, stat_send, stat_recv, x_send, x_recv, h_send, h_recv,
):
    tm = lax.axis_index("tm")
    z = lax.axis_index("rows")
    last_tm = lax.axis_size("tm") - 1
    last_z = lax.axis_size("rows") - 1
    here = {"y": tm // 8, "x": (tm // 2) % 4, "core": tm % 2, "z": z}

    def partner(axes, offset):
        there = dict(here)
        for a, o in zip(axes, offset):
            there[a] = lax.rem(here[a] + o, SIZES[a])
        return ((there["y"] * 4 + there["x"]) * 2 + there["core"], there["z"])

    barrier = pltpu.get_barrier_semaphore()
    stage_partners = [[partner(axes, o) for o in offsets(axes)] for axes in STAGES]

    loads = [
        pltpu.make_async_copy(src, dst, load_sem.at[i])
        for i, (src, dst) in enumerate(
            [
                (x_hbm, xr.at[2:6, 1:9]),
                (gain_in_hbm, gain_in),
                (shift_in_hbm, shift_in),
                (short_hbm, short),
                (w1_hbm, w1),
                (gain_mid_hbm, gain_mid),
                (shift_mid_hbm, shift_mid),
                (w2_hbm, w2),
            ]
        )
    ]
    for load in loads:
        load.start()

    for target in itertools.chain(*stage_partners):
        pl.semaphore_signal(barrier, inc=1, device_id=target, device_id_type=MESH)

    def greet(ok, target):
        @pl.when(ok)
        def _():
            pl.semaphore_signal(barrier, inc=1, device_id=target, device_id_type=MESH)

    greet(tm > 0, (tm - 1, z))
    greet((tm > 0) & (z > 0), (tm - 1, z - 1))
    greet((tm > 0) & (z < last_z), (tm - 1, z + 1))

    has_next = tm < last_tm
    has_prev = tm > 0
    has_above = z > 0
    has_below = z < last_z

    def halo_copies(src, ext, send, recv, parts):
        frames = {"all": (0, 4), "late": (2, 4), "early": (0, 2)}
        made = []
        for part in parts:
            kind, span, slot = part
            lo, hi = frames[span]
            if kind == "next":
                made.append(
                    (has_next, has_prev, src(2, 4, 0, 8), ext.at[0:2, 1:9], (tm + 1, z), slot)
                )
            elif kind == "down":
                made.append(
                    (has_below, has_above, src(lo, hi, 7, 8), ext.at[2 + lo : 2 + hi, 0:1],
                     (tm, z + 1), slot)
                )
            elif kind == "up":
                made.append(
                    (has_above, has_below, src(lo, hi, 0, 1), ext.at[2 + lo : 2 + hi, 9:10],
                     (tm, z - 1), slot)
                )
            elif kind == "next_down":
                made.append(
                    (has_next & has_below, has_prev & has_above, src(2, 4, 7, 8),
                     ext.at[0:2, 0:1], (tm + 1, z + 1), slot)
                )
            else:
                made.append(
                    (has_next & has_above, has_prev & has_below, src(2, 4, 0, 1),
                     ext.at[0:2, 9:10], (tm + 1, z - 1), slot)
                )
        copies = []
        for sends, gets, source, target, device, slot in made:
            copy = pltpu.make_async_remote_copy(
                src_ref=source, dst_ref=target, send_sem=send.at[slot], recv_sem=recv.at[slot],
                device_id=device, device_id_type=MESH,
            )
            copies.append((sends, gets, copy))
        return copies

    def start(copies):
        for sends, _, copy in copies:
            pl.when(sends)(copy.start)

    def wait_sent(copies):
        for sends, _, copy in copies:
            pl.when(sends)(copy.wait_send)

    def wait_received(copies):
        for _, gets, copy in copies:
            pl.when(gets)(copy.wait_recv)

    def stat_copies(which, stage):
        buffer = (stat_in_a, stat_in_b)[stage]
        return [
            pltpu.make_async_remote_copy(
                src_ref=stat_out.at[which, stage], dst_ref=buffer.at[which, i],
                send_sem=stat_send.at[which, stage], recv_sem=stat_recv.at[which, stage],
                device_id=target, device_id_type=MESH,
            )
            for i, target in enumerate(stage_partners[stage])
        ]

    def exchange(which, packed, count, meanwhile):
        for stage in range(2):
            buffer = (stat_in_a, stat_in_b)[stage]
            stat_out[which, stage] = packed
            for copy in stat_copies(which, stage):
                copy.start()
            meanwhile(stage)
            pltpu.make_async_copy(
                buffer.at[which], buffer.at[which], stat_recv.at[which, stage]
            ).wait()
            packed = combined(packed, buffer[which], count)
            count = count * (buffer.shape[1] + 1)
        return packed, count

    def coefficients(packed, count, channels, gain, shift):
        mean, spread = unpacked(packed, channels)
        inverse = lax.rsqrt(spread * (1.0 / count) + EPSILON)
        return to_lanes(mean), 0.5 * gain[...] * to_lanes(inverse), 0.5 * shift[...]

    def activate_own(raw, out, mean, scale, shift):
        def body(i, carry):
            activate_slab(raw, out, 2 + i // ROWS, 1 + i % ROWS, mean, scale, shift)
            return carry

        lax.fori_loop(0, FRAMES * ROWS, body, 0, unroll=2)

    def activate_edges(raw, out, lo, hi, mean, scale, shift):
        for row, ok in ((0, has_above), (9, has_below)):

            @pl.when(ok)
            def _():
                def body(f, carry):
                    activate_slab(raw, out, f, row, mean, scale, shift)
                    return carry

                lax.fori_loop(lo, hi, body, 0)

            @pl.when(jnp.logical_not(ok))
            def _():
                out[lo:hi, row] = jnp.zeros((hi - lo, COLS, out.shape[-1]), BF16)

    def activate_past(raw, out, mean, scale, shift):
        @pl.when(has_prev)
        def _():
            def body(i, carry):
                activate_slab(raw, out, i // ROWS, 1 + i % ROWS, mean, scale, shift)
                return carry

            lax.fori_loop(0, 2 * ROWS, body, 0, unroll=2)
            activate_edges(raw, out, 0, 2, mean, scale, shift)

        @pl.when(jnp.logical_not(has_prev))
        def _():
            def body(r, carry):
                out[0, r] = out[2, r]
                out[1, r] = out[2, r]
                return carry

            lax.fori_loop(0, ROWS + 2, body, 0)

    x_copies = halo_copies(
        lambda f0, f1, r0, r1: x_hbm.at[f0:f1, r0:r1], xr, x_send, x_recv,
        [("down", "all", 0), ("up", "all", 1), ("next", "all", 2),
         ("next_down", "all", 3), ("next_up", "all", 4)],
    )

    def own_hidden(f0, f1, r0, r1):
        return hr.at[2 + f0 : 2 + f1, 1 + r0 : 1 + r1]

    h_late = halo_copies(
        own_hidden, hr, h_send, h_recv,
        [("next", "all", 0), ("next_down", "all", 1), ("next_up", "all", 2),
         ("down", "late", 3), ("up", "late", 4)],
    )
    h_early = halo_copies(
        own_hidden, hr, h_send, h_recv, [("down", "early", 5), ("up", "early", 6)]
    )

    loads[0].wait()
    packed = local_statistics(xr)
    pl.semaphore_wait(
        barrier,
        sum(len(p) for p in stage_partners)
        + has_next.astype(jnp.int32)
        + (has_next & has_above).astype(jnp.int32)
        + (has_next & has_below).astype(jnp.int32),
    )

    def during_first(stage):
        if stage == 0:
            loads[3].wait()
            skip[...] = jnp.dot(
                xr[2:6, 1:9].reshape(CELLS, xr.shape[-1]), short[...], preferred_element_type=F32
            )
        if stage == 1:
            start(x_copies)

    packed, count = exchange(0, packed, CELLS * (xr.shape[-1] // GROUPS), during_first)
    loads[1].wait()
    loads[2].wait()
    mean, scale, shift = coefficients(packed, count, xr.shape[-1], gain_in, shift_in)
    activate_own(xr, xa, mean, scale, shift)
    wait_received(x_copies[:2])
    activate_edges(xr, xa, 2, 6, mean, scale, shift)
    loads[4].wait()
    hidden = convolve(xa, w1, acc, 2, 2)
    hr[4:6, 1:9] = hidden.reshape(2, ROWS, COLS, hidden.shape[-1]).astype(BF16)
    start(h_late)
    wait_received(x_copies[2:])
    activate_past(xr, xa, mean, scale, shift)
    hidden = convolve(xa, w1, acc, 0, 2)
    hr[2:4, 1:9] = hidden.reshape(2, ROWS, COLS, hidden.shape[-1]).astype(BF16)

    packed = local_statistics(hr)

    def during_second(stage):
        if stage == 0:
            start(h_early)

    packed, count = exchange(1, packed, CELLS * (hr.shape[-1] // GROUPS), during_second)
    loads[5].wait()
    loads[6].wait()
    mean, scale, shift = coefficients(packed, count, hr.shape[-1], gain_mid, shift_mid)
    activate_own(hr, ha, mean, scale, shift)
    wait_received(h_late)
    wait_received(h_early)
    activate_edges(hr, ha, 2, 6, mean, scale, shift)
    activate_past(hr, ha, mean, scale, shift)
    loads[7].wait()
    decoded = convolve(ha, w2, acc, 0, 4) + skip[...]
    out_ref[...] = decoded.reshape(out_ref.shape).astype(BF16)

    wait_sent(x_copies)
    wait_sent(h_late)
    wait_sent(h_early)
    for which in range(2):
        for stage in range(2):
            buffer = (stat_in_a, stat_in_b)[stage]
            pltpu.make_async_copy(
                buffer.at[which], buffer.at[which], stat_send.at[which, stage]
            ).wait()


def per_device(features, gain_in, shift_in, conv_in, gain_mid, shift_mid, conv_out, shortcut):
    c_in = features.shape[-1]
    c_out = shortcut.shape[-1]
    members = [len(offsets(axes)) for axes in STAGES]
    whole = pl.BlockSpec(memory_space=pl.ANY)
    return pl.pallas_call(
        kernel,
        out_shape=jax.ShapeDtypeStruct((FRAMES, ROWS, COLS, c_out), BF16),
        in_specs=[whole] * 8,
        out_specs=pl.BlockSpec(memory_space=pltpu.VMEM),
        scratch_shapes=[
            pltpu.VMEM((FRAMES + 2, ROWS + 2, COLS, c_in), BF16),
            pltpu.VMEM((FRAMES + 2, ROWS + 2, COLS, c_in), BF16),
            pltpu.VMEM((FRAMES + 2, ROWS + 2, COLS, c_out), BF16),
            pltpu.VMEM((FRAMES + 2, ROWS + 2, COLS, c_out), BF16),
            pltpu.VMEM(conv_in.shape, BF16),
            pltpu.VMEM(conv_out.shape, BF16),
            pltpu.VMEM(shortcut.shape, BF16),
            pltpu.VMEM((3, CELLS, c_out), F32),
            pltpu.VMEM((CELLS, c_out), F32),
            pltpu.VMEM((1, c_in), F32),
            pltpu.VMEM((1, c_in), F32),
            pltpu.VMEM((1, c_out), F32),
            pltpu.VMEM((1, c_out), F32),
            pltpu.VMEM((2, 2, 1, 128), F32),
            pltpu.VMEM((2, members[0], 1, 128), F32),
            pltpu.VMEM((2, members[1], 1, 128), F32),
            pltpu.SemaphoreType.DMA((8,)),
            pltpu.SemaphoreType.DMA((2, 2)),
            pltpu.SemaphoreType.DMA((2, 2)),
            pltpu.SemaphoreType.DMA((5,)),
            pltpu.SemaphoreType.DMA((5,)),
            pltpu.SemaphoreType.DMA((7,)),
            pltpu.SemaphoreType.DMA((7,)),
        ],
        compiler_params=pltpu.CompilerParams(
            collective_id=0, has_side_effects=True, vmem_limit_bytes=60 * 2**20
        ),
        name="residual_block",
    )(
        features, gain_in.reshape(1, -1), shift_in.reshape(1, -1), conv_in,
        gain_mid.reshape(1, -1), shift_mid.reshape(1, -1), conv_out, shortcut,
    )


def solution(mesh):
    return jax.shard_map(
        per_device,
        mesh=mesh,
        in_specs=(P("tm", "rows", None, None), P(), P(), P(), P(), P(), P(), P()),
        out_specs=P("tm", "rows", None, None),
        check_vma=False,
    )
```

```python
import itertools

import jax
import jax.numpy as jnp
from jax import lax
from jax.experimental import pallas as pl
from jax.experimental.pallas import tpu as pltpu
from jax.sharding import PartitionSpec as P

GROUPS = 32
FRAMES = 4
ROWS = 8
COLS = 32
CELLS = FRAMES * ROWS * COLS
EPSILON = 1e-06
F32 = jnp.float32
BF16 = jnp.bfloat16
MESH = pl.DeviceIdType.MESH
SIZES = {"y": 4, "x": 4, "core": 2, "z": 8}
STAGES = ((("z", "core"), ("y", "x")), (("core",), ("y", "x", "z")))
HOPS = {2: (0, 1), 4: (0, 1, 2, 1), 8: (0, 1, 2, 3, 4, 3, 2, 1)}


def offsets(axes):
    every = itertools.product(*[range(SIZES[a]) for a in axes])
    moved = [o for o in every if any(o)]
    return sorted(moved, key=lambda o: -sum(HOPS[SIZES[a]][i] for a, i in zip(axes, o)))


def group_sum(values, width):
    lane = lax.broadcasted_iota(jnp.int32, values.shape, 1)
    step = 1
    while step < width:
        up = pltpu.roll(values, 128 - step, 1)
        down = pltpu.roll(values, step, 1)
        values = values + jnp.where((lane // step) % 2 == 0, up, down)
        step *= 2
    return values


def to_rows(values):
    return jnp.concatenate([values[:, i : i + 128] for i in range(0, values.shape[1], 128)], axis=0)


def to_lanes(values):
    return jnp.concatenate([values[i : i + 1, :] for i in range(values.shape[0])], axis=1)


def local_statistics(ext):
    channels = ext.shape[-1]
    width = channels // GROUPS
    rows = channels // 128

    def slab(i):
        return ext[2 + i // ROWS, 1 + i % ROWS].astype(F32)

    def add_up(i, total):
        return total + slab(i).reshape(COLS // 8, 8, channels).sum(0)

    zero = jnp.zeros((8, channels), F32)
    total = lax.fori_loop(0, FRAMES * ROWS, add_up, zero, unroll=4).sum(0, keepdims=True)
    mean = group_sum(to_rows(total), width) * (1.0 / (CELLS * width))
    wide_mean = to_lanes(mean)

    def add_square(i, total):
        return total + jnp.square(slab(i) - wide_mean).reshape(COLS // 8, 8, channels).sum(0)

    spread = lax.fori_loop(0, FRAMES * ROWS, add_square, zero, unroll=4).sum(0, keepdims=True)
    spread = group_sum(to_rows(spread), width)
    lane = lax.broadcasted_iota(jnp.int32, (1, 128), 1)
    packed = jnp.zeros((1, 128), F32)
    for r in range(rows):
        both = jnp.where(lane % 4 < 2, mean[r : r + 1], spread[r : r + 1])
        packed = packed + jnp.where((lane % width) // 4 == r, both, 0.0)
    return packed


def combined(own, others, count):
    members = others.shape[0] + 1
    lane = lax.broadcasted_iota(jnp.int32, (1, 128), 1)
    total = own + jnp.sum(others, axis=0)
    mean = total * (1.0 / members)
    deviation = jnp.square(own - mean) + jnp.sum(jnp.square(others - mean[None]), axis=0)
    moved = pltpu.roll(deviation, 2, 1)
    return jnp.where(lane % 4 < 2, mean, total + moved * float(count))


def unpacked(packed, channels):
    width = channels // GROUPS
    rows = channels // 128
    shape = (2 * rows, 128)
    lane = lax.broadcasted_iota(jnp.int32, shape, 1)
    row = lax.broadcasted_iota(jnp.int32, shape, 0)
    wanted = jnp.where(row < rows, 4 * row, 4 * (row - rows) + 2)
    picked = jnp.where(lane % width == wanted, jnp.broadcast_to(packed, shape), 0.0)
    spread = group_sum(picked, width)
    return spread[:rows], spread[rows:]


def activate_slab(raw, out, frame, row, mean, scale, shift):
    v = (raw[frame, row].astype(F32) - mean) * scale + shift
    out[frame, row % 2, row // 2] = (v + v * jnp.tanh(v)).astype(BF16)


def transform_weights(weights, sums):
    depth = weights.shape[3]
    step = 64

    def body(i, carry):
        tap, part = i // (depth // step), i % (depth // step)
        a, e = tap // 3, tap % 3
        k = pl.ds(pl.multiple_of(part * step, step), step)
        outer = weights[a, 0, e, k].astype(F32) + weights[a, 2, e, k].astype(F32)
        middle = weights[a, 1, e, k].astype(F32)
        sums[a, 0, e, k] = (outer + middle).astype(BF16)
        sums[a, 1, e, k] = (outer - middle).astype(BF16)
        return carry

    lax.fori_loop(0, 9 * (depth // step), body, 0)


def convolve(act, weights, sums, acc, hold, first_frame, frames):
    channels = act.shape[-1]
    width = weights.shape[-1]
    half = ROWS // 2
    cells = frames * half * COLS

    def one_column_tap(e, carry):
        def rows(a, parity, k):
            frame = first_frame + a
            return act[frame : frame + frames, parity, k : k + half].reshape(cells, channels)

        inputs = [
            lambda a: rows(a, 0, 0) - rows(a, 0, 1),
            lambda a: rows(a, 1, 0) + rows(a, 0, 1),
            lambda a: rows(a, 0, 1) - rows(a, 1, 0),
            lambda a: rows(a, 1, 0) - rows(a, 1, 1),
        ]
        matrices = [weights[:, 0, e], sums[:, 0, e], sums[:, 1, e], weights[:, 2, e]]
        for i in range(4):
            taps = jnp.concatenate([inputs[i](a) for a in range(3)], axis=-1)
            acc[e, i, 0:cells] = jnp.dot(
                taps, matrices[i].reshape(3 * channels, width), preferred_element_type=F32
            )
        return carry

    lax.fori_loop(0, 3, one_column_tap, 0)

    def row_of(parity, e):
        if parity == 0:
            return acc[e, 0, 0:cells] + 0.5 * (acc[e, 1, 0:cells] + acc[e, 2, 0:cells])
        return 0.5 * (acc[e, 1, 0:cells] - acc[e, 2, 0:cells]) - acc[e, 3, 0:cells]

    for parity in range(2):
        left, middle, right = (row_of(parity, e) for e in range(3))
        col = lax.broadcasted_iota(jnp.int32, left.shape, 0) % COLS
        from_left = jnp.where(col == 0, 0.0, pltpu.roll(left, 1, 0))
        from_right = jnp.where(col == COLS - 1, 0.0, pltpu.roll(right, cells - 1, 0))
        summed = middle + from_left + from_right
        for f in range(frames):
            for k in range(half):
                start = (f * half + k) * COLS
                hold(first_frame + f, 2 * k + parity, summed[start : start + COLS])


def kernel(
    x_hbm, gain_in_hbm, shift_in_hbm, w1_hbm, gain_mid_hbm, shift_mid_hbm, w2_hbm, short_hbm,
    out_ref,
    xr, xa, hr, ha, w1, s1, w2, s2, short, acc, skip, gain_in, shift_in, gain_mid, shift_mid,
    stat_out, stat_in_a, stat_in_b, stat_in_c, stat_in_d,
    load_sem, stat_send, stat_recv, x_send, x_recv, h_send, h_recv,
):
    tm = lax.axis_index("tm")
    z = lax.axis_index("rows")
    last_tm = lax.axis_size("tm") - 1
    last_z = lax.axis_size("rows") - 1
    here = {"y": tm // 8, "x": (tm // 2) % 4, "core": tm % 2, "z": z}

    def partner(axes, offset):
        there = dict(here)
        for a, o in zip(axes, offset):
            there[a] = lax.rem(here[a] + o, SIZES[a])
        return ((there["y"] * 4 + there["x"]) * 2 + there["core"], there["z"])

    barrier = pltpu.get_barrier_semaphore()
    stage_partners = [
        [[partner(axes, o) for o in offsets(axes)] for axes in stages] for stages in STAGES
    ]
    stat_in = ((stat_in_a, stat_in_b), (stat_in_c, stat_in_d))

    loads = [
        pltpu.make_async_copy(src, dst, load_sem.at[i])
        for i, (src, dst) in enumerate(
            [
                (x_hbm, xr.at[2:6, 1:9]),
                (gain_in_hbm, gain_in),
                (shift_in_hbm, shift_in),
                (short_hbm, short),
                (w1_hbm, w1),
                (gain_mid_hbm, gain_mid),
                (shift_mid_hbm, shift_mid),
                (w2_hbm, w2),
            ]
        )
    ]
    loads[0].start()

    for target in itertools.chain(*stage_partners[0]):
        pl.semaphore_signal(barrier, inc=1, device_id=target, device_id_type=MESH)

    def greet(ok, target):
        @pl.when(ok)
        def _():
            pl.semaphore_signal(barrier, inc=1, device_id=target, device_id_type=MESH)

    greet(tm > 0, (tm - 1, z))
    greet((tm > 0) & (z > 0), (tm - 1, z - 1))
    greet((tm > 0) & (z < last_z), (tm - 1, z + 1))

    has_next = tm < last_tm
    has_prev = tm > 0
    has_above = z > 0
    has_below = z < last_z

    def halo_copies(src, ext, send, recv, parts):
        frames = {"all": (0, 4), "late": (2, 4), "early": (0, 2)}
        made = []
        for part in parts:
            kind, span, slot = part
            lo, hi = frames[span]
            if kind == "next":
                made.append(
                    (has_next, has_prev, src(2, 4, 0, 8), ext.at[0:2, 1:9], (tm + 1, z), slot)
                )
            elif kind == "down":
                made.append(
                    (has_below, has_above, src(lo, hi, 7, 8), ext.at[2 + lo : 2 + hi, 0:1],
                     (tm, z + 1), slot)
                )
            elif kind == "up":
                made.append(
                    (has_above, has_below, src(lo, hi, 0, 1), ext.at[2 + lo : 2 + hi, 9:10],
                     (tm, z - 1), slot)
                )
            elif kind == "next_down":
                made.append(
                    (has_next & has_below, has_prev & has_above, src(2, 4, 7, 8),
                     ext.at[0:2, 0:1], (tm + 1, z + 1), slot)
                )
            else:
                made.append(
                    (has_next & has_above, has_prev & has_below, src(2, 4, 0, 1),
                     ext.at[0:2, 9:10], (tm + 1, z - 1), slot)
                )
        copies = []
        for sends, gets, source, target, device, slot in made:
            copy = pltpu.make_async_remote_copy(
                src_ref=source, dst_ref=target, send_sem=send.at[slot], recv_sem=recv.at[slot],
                device_id=device, device_id_type=MESH,
            )
            copies.append((sends, gets, copy))
        return copies

    def start(copies):
        for sends, _, copy in copies:
            pl.when(sends)(copy.start)

    def wait_sent(copies):
        for sends, _, copy in copies:
            pl.when(sends)(copy.wait_send)

    def wait_received(copies):
        for _, gets, copy in copies:
            pl.when(gets)(copy.wait_recv)

    def stat_copies(which, stage):
        return [
            pltpu.make_async_remote_copy(
                src_ref=stat_out.at[which, stage], dst_ref=stat_in[which][stage].at[i],
                send_sem=stat_send.at[which, stage], recv_sem=stat_recv.at[which, stage],
                device_id=target, device_id_type=MESH,
            )
            for i, target in enumerate(stage_partners[which][stage])
        ]

    def exchange(which, packed, count, meanwhile):
        for stage in range(2):
            buffer = stat_in[which][stage]
            stat_out[which, stage] = packed
            for copy in stat_copies(which, stage):
                copy.start()
            meanwhile(stage)
            pltpu.make_async_copy(buffer, buffer, stat_recv.at[which, stage]).wait()
            packed = combined(packed, buffer[...], count)
            count = count * (buffer.shape[0] + 1)
        return packed, count

    def coefficients(packed, count, channels, gain, shift):
        mean, spread = unpacked(packed, channels)
        inverse = lax.rsqrt(spread * (1.0 / count) + EPSILON)
        return to_lanes(mean), 0.5 * gain[...] * to_lanes(inverse), 0.5 * shift[...]

    def activate_own(raw, out, mean, scale, shift):
        def body(i, carry):
            activate_slab(raw, out, 2 + i // ROWS, 1 + i % ROWS, mean, scale, shift)
            return carry

        lax.fori_loop(0, FRAMES * ROWS, body, 0, unroll=2)

    def activate_edges(raw, out, lo, hi, mean, scale, shift):
        for row, ok in ((0, has_above), (9, has_below)):

            @pl.when(ok)
            def _():
                def body(f, carry):
                    activate_slab(raw, out, f, row, mean, scale, shift)
                    return carry

                lax.fori_loop(lo, hi, body, 0)

            @pl.when(jnp.logical_not(ok))
            def _():
                out[lo:hi, row % 2, row // 2] = jnp.zeros((hi - lo, COLS, out.shape[-1]), BF16)

    def activate_past(raw, out, mean, scale, shift):
        @pl.when(has_prev)
        def _():
            def body(i, carry):
                activate_slab(raw, out, i // ROWS, 1 + i % ROWS, mean, scale, shift)
                return carry

            lax.fori_loop(0, 2 * ROWS, body, 0, unroll=2)
            activate_edges(raw, out, 0, 2, mean, scale, shift)

        @pl.when(jnp.logical_not(has_prev))
        def _():
            def body(r, carry):
                out[0, r % 2, r // 2] = out[2, r % 2, r // 2]
                out[1, r % 2, r // 2] = out[2, r % 2, r // 2]
                return carry

            lax.fori_loop(0, ROWS + 2, body, 0)

    x_copies = halo_copies(
        lambda f0, f1, r0, r1: x_hbm.at[f0:f1, r0:r1], xr, x_send, x_recv,
        [("down", "all", 0), ("up", "all", 1), ("next", "all", 2),
         ("next_down", "all", 3), ("next_up", "all", 4)],
    )

    def own_hidden(f0, f1, r0, r1):
        return hr.at[2 + f0 : 2 + f1, 1 + r0 : 1 + r1]

    h_late = halo_copies(
        own_hidden, hr, h_send, h_recv,
        [("next", "all", 0), ("next_down", "all", 1), ("next_up", "all", 2),
         ("down", "late", 3), ("up", "late", 4)],
    )
    h_early = halo_copies(
        own_hidden, hr, h_send, h_recv, [("down", "early", 5), ("up", "early", 6)]
    )

    loads[0].wait()
    for load in loads[1:]:
        load.start()
    packed = local_statistics(xr)
    pl.semaphore_wait(
        barrier,
        sum(len(p) for p in stage_partners[0])
        + has_next.astype(jnp.int32)
        + (has_next & has_above).astype(jnp.int32)
        + (has_next & has_below).astype(jnp.int32),
    )

    def during_first(stage):
        if stage == 0:
            loads[3].wait()
            skip[...] = jnp.dot(
                xr[2:6, 1:9].reshape(CELLS, xr.shape[-1]), short[...], preferred_element_type=F32
            )
            loads[7].wait()
            transform_weights(w2, s2)
        if stage == 1:
            start(x_copies)
            loads[4].wait()
            transform_weights(w1, s1)

    packed, count = exchange(0, packed, CELLS * (xr.shape[-1] // GROUPS), during_first)
    loads[1].wait()
    loads[2].wait()
    mean, scale, shift = coefficients(packed, count, xr.shape[-1], gain_in, shift_in)
    activate_own(xr, xa, mean, scale, shift)
    wait_received(x_copies[:2])
    activate_edges(xr, xa, 2, 6, mean, scale, shift)

    def hold_hidden(frame, row, values):
        hr[2 + frame, 1 + row] = values.astype(BF16)

    convolve(xa, w1, s1, acc, hold_hidden, 2, 2)
    start(h_late)
    wait_received(x_copies[2:])
    activate_past(xr, xa, mean, scale, shift)
    convolve(xa, w1, s1, acc, hold_hidden, 0, 2)

    packed = local_statistics(hr)

    def during_second(stage):
        if stage == 0:
            start(h_early)

    packed, count = exchange(1, packed, CELLS * (hr.shape[-1] // GROUPS), during_second)
    loads[5].wait()
    loads[6].wait()
    mean, scale, shift = coefficients(packed, count, hr.shape[-1], gain_mid, shift_mid)
    activate_own(hr, ha, mean, scale, shift)
    wait_received(h_late)
    wait_received(h_early)
    activate_edges(hr, ha, 2, 6, mean, scale, shift)
    activate_past(hr, ha, mean, scale, shift)

    def hold_decoded(frame, row, values):
        cell = (frame * ROWS + row) * COLS
        out_ref[frame, row] = (values + skip[cell : cell + COLS]).astype(BF16)

    convolve(ha, w2, s2, acc, hold_decoded, 0, 4)

    wait_sent(x_copies)
    wait_sent(h_late)
    wait_sent(h_early)
    for which in range(2):
        for stage in range(2):
            buffer = stat_in[which][stage]
            pltpu.make_async_copy(buffer, buffer, stat_send.at[which, stage]).wait()


def per_device(features, gain_in, shift_in, conv_in, gain_mid, shift_mid, conv_out, shortcut):
    c_in = features.shape[-1]
    c_out = shortcut.shape[-1]
    members = [len(offsets(axes)) for stages in STAGES for axes in stages]
    half = (ROWS + 2) // 2
    whole = pl.BlockSpec(memory_space=pl.ANY)
    return pl.pallas_call(
        kernel,
        out_shape=pltpu.VMEM((FRAMES, ROWS, COLS, c_out), BF16),
        in_specs=[whole] * 8,
        out_specs=pl.BlockSpec(memory_space=pltpu.VMEM),
        scratch_shapes=[
            pltpu.VMEM((FRAMES + 2, ROWS + 2, COLS, c_in), BF16),
            pltpu.VMEM((FRAMES + 2, 2, half, COLS, c_in), BF16),
            pltpu.VMEM((FRAMES + 2, ROWS + 2, COLS, c_out), BF16),
            pltpu.VMEM((FRAMES + 2, 2, half, COLS, c_out), BF16),
            pltpu.VMEM(conv_in.shape, BF16),
            pltpu.VMEM((3, 2, 3, c_in, c_out), BF16),
            pltpu.VMEM(conv_out.shape, BF16),
            pltpu.VMEM((3, 2, 3, c_out, c_out), BF16),
            pltpu.VMEM(shortcut.shape, BF16),
            pltpu.VMEM((3, 4, CELLS // 2, c_out), F32),
            pltpu.VMEM((CELLS, c_out), F32),
            pltpu.VMEM((1, c_in), F32),
            pltpu.VMEM((1, c_in), F32),
            pltpu.VMEM((1, c_out), F32),
            pltpu.VMEM((1, c_out), F32),
            pltpu.VMEM((2, 2, 1, 128), F32),
            *[pltpu.VMEM((count, 1, 128), F32) for count in members],
            pltpu.SemaphoreType.DMA((8,)),
            pltpu.SemaphoreType.DMA((2, 2)),
            pltpu.SemaphoreType.DMA((2, 2)),
            pltpu.SemaphoreType.DMA((5,)),
            pltpu.SemaphoreType.DMA((5,)),
            pltpu.SemaphoreType.DMA((7,)),
            pltpu.SemaphoreType.DMA((7,)),
        ],
        compiler_params=pltpu.CompilerParams(
            collective_id=0, has_side_effects=True, vmem_limit_bytes=60 * 2**20
        ),
        name="residual_block",
    )(
        features, gain_in.reshape(1, -1), shift_in.reshape(1, -1), conv_in,
        gain_mid.reshape(1, -1), shift_mid.reshape(1, -1), conv_out, shortcut,
    )


def solution(mesh):
    return jax.shard_map(
        per_device,
        mesh=mesh,
        in_specs=(P("tm", "rows", None, None), P(), P(), P(), P(), P(), P(), P()),
        out_specs=P("tm", "rows", None, None),
        check_vma=False,
    )
```

```python
import itertools

import jax
import jax.numpy as jnp
from jax import lax
from jax.experimental import pallas as pl
from jax.experimental.pallas import tpu as pltpu
from jax.sharding import PartitionSpec as P

GROUPS = 32
FRAMES = 4
ROWS = 8
COLS = 32
CELLS = FRAMES * ROWS * COLS
EPSILON = 1e-06
F32 = jnp.float32
BF16 = jnp.bfloat16
MESH = pl.DeviceIdType.MESH
SIZES = {"y": 4, "x": 4, "core": 2, "z": 8}
UNROLL = 8
STAGES = ((("z", "core"), ("y", "x")), (("core",), ("y", "x", "z")))
HOPS = {2: (0, 1), 4: (0, 1, 2, 1), 8: (0, 1, 2, 3, 4, 3, 2, 1)}


def offsets(axes):
    every = itertools.product(*[range(SIZES[a]) for a in axes])
    moved = [o for o in every if any(o)]
    return sorted(moved, key=lambda o: -sum(HOPS[SIZES[a]][i] for a, i in zip(axes, o)))


def group_sum(values, width):
    lane = lax.broadcasted_iota(jnp.int32, values.shape, 1)
    step = 1
    while step < width:
        up = pltpu.roll(values, 128 - step, 1)
        down = pltpu.roll(values, step, 1)
        values = values + jnp.where((lane // step) % 2 == 0, up, down)
        step *= 2
    return values


def to_rows(values):
    return jnp.concatenate([values[:, i : i + 128] for i in range(0, values.shape[1], 128)], axis=0)


def to_lanes(values):
    return jnp.concatenate([values[i : i + 1, :] for i in range(values.shape[0])], axis=1)


def group_pivot(ext, frame):
    channels = ext.shape[-1]
    width = channels // GROUPS
    cell = to_rows(ext[frame, 1].astype(F32)[0:1])
    lane = lax.broadcasted_iota(jnp.int32, cell.shape, 1)
    return group_sum(jnp.where(lane % width == 0, cell, 0.0), width)


def add_up(ext, first, frames, pivot, sums):
    channels = ext.shape[-1]
    slabs = 4

    def body(i, carry):
        total, spread = carry
        for j in range(slabs):
            n = i * slabs + j
            moved = ext[first + n // ROWS, 1 + n % ROWS].astype(F32) - pivot
            parts = moved.reshape(COLS // 8, 8, channels)
            total = total + parts.sum(0)
            spread = spread + jnp.square(parts).sum(0)
        return total, spread

    return lax.fori_loop(0, frames * ROWS // slabs, body, sums)


def no_sums(channels):
    return jnp.zeros((8, channels), F32), jnp.zeros((8, channels), F32)


def packed_statistics(pivot, sums):
    total, spread = sums
    channels = total.shape[-1]
    width = channels // GROUPS
    rows = channels // 128
    both = jnp.concatenate(
        [to_rows(total.sum(0, keepdims=True)), to_rows(spread.sum(0, keepdims=True))], axis=0
    )
    both = group_sum(both, width)
    offset = both[:rows] * (1.0 / (CELLS * width))
    mean = pivot + offset
    spread = both[rows:] - both[:rows] * offset
    lane = lax.broadcasted_iota(jnp.int32, (1, 128), 1)
    packed = jnp.zeros((1, 128), F32)
    for r in range(rows):
        pair = jnp.where(lane % 4 < 2, mean[r : r + 1], spread[r : r + 1])
        packed = packed + jnp.where((lane % width) // 4 == r, pair, 0.0)
    return packed


def combined(own, others, count):
    held = others.shape[0] * others.shape[1]
    full = held % 2 == 0
    members = held if full else held + 1
    lane = lax.broadcasted_iota(jnp.int32, (1, 128), 1)

    def over_all(values):
        return jnp.sum(jnp.sum(values, axis=0), axis=0, keepdims=True)

    total = over_all(others) if full else own + over_all(others)
    mean = total * (1.0 / members)
    deviation = over_all(jnp.square(others - mean[None]))
    if not full:
        deviation = deviation + jnp.square(own - mean)
    moved = pltpu.roll(deviation, 2, 1)
    return jnp.where(lane % 4 < 2, mean, total + moved * float(count)), members


def unpacked(packed, channels):
    width = channels // GROUPS
    rows = channels // 128
    shape = (2 * rows, 128)
    lane = lax.broadcasted_iota(jnp.int32, shape, 1)
    row = lax.broadcasted_iota(jnp.int32, shape, 0)
    wanted = jnp.where(row < rows, 4 * row, 4 * (row - rows) + 2)
    picked = jnp.where(lane % width == wanted, jnp.broadcast_to(packed, shape), 0.0)
    spread = group_sum(picked, width)
    return spread[:rows], spread[rows:]


def activate_slab(raw, out, frame, row, mean, scale, shift):
    v = (raw[frame, row].astype(F32) - mean) * scale + shift
    out[frame, row % 2, row // 2] = (v + v * jnp.tanh(v)).astype(BF16)


def transform_weights(weights, sums):
    depth = weights.shape[3]
    step = 64

    def body(i, carry):
        tap, part = i // (depth // step), i % (depth // step)
        a, e = tap // 3, tap % 3
        k = pl.ds(pl.multiple_of(part * step, step), step)
        outer = 0.5 * (weights[a, 0, e, k].astype(F32) + weights[a, 2, e, k].astype(F32))
        middle = 0.5 * weights[a, 1, e, k].astype(F32)
        sums[a, 0, e, k] = (outer + middle).astype(BF16)
        sums[a, 1, e, k] = (outer - middle).astype(BF16)
        return carry

    lax.fori_loop(0, 9 * (depth // step), body, 0)


def convolve(act, weights, sums, acc, hold, first_frame, frames):
    channels = act.shape[-1]
    width = weights.shape[-1]
    half = ROWS // 2
    cells = frames * half * COLS
    col = lax.broadcasted_iota(jnp.int32, (COLS, width), 0)

    def rows(a, parity, k):
        frame = first_frame + a
        return act[frame : frame + frames, parity, k : k + half].reshape(cells, channels)

    inputs = [
        lambda a: rows(a, 0, 0) - rows(a, 0, 1),
        lambda a: rows(a, 1, 0) + rows(a, 0, 1),
        lambda a: rows(a, 0, 1) - rows(a, 1, 0),
        lambda a: rows(a, 1, 0) - rows(a, 1, 1),
    ]

    def one_column_tap(e):
        matrices = [weights[:, 0, e], sums[:, 0, e], sums[:, 1, e], weights[:, 2, e]]
        for i in range(4):
            taps = jnp.concatenate([inputs[i](a) for a in range(3)], axis=-1)
            acc[e, i, 0:cells] = jnp.dot(
                taps, matrices[i].reshape(3 * channels, width), preferred_element_type=F32
            )

    def pair_of_rows(e, slab):
        m = [acc[e, i, slab] for i in range(4)]
        return m[0] + (m[1] + m[2]), (m[1] - m[2]) - m[3]

    places = [
        (f, k, slice((f * half + k) * COLS, (f * half + k + 1) * COLS))
        for f in range(frames)
        for k in range(half)
    ]
    one_column_tap(0)
    one_column_tap(1)
    for _, _, slab in places:
        left, middle = pair_of_rows(0, slab), pair_of_rows(1, slab)
        for parity in range(2):
            from_left = jnp.where(col == 0, 0.0, pltpu.roll(left[parity], 1, 0))
            acc[0, parity, slab] = middle[parity] + from_left
    one_column_tap(2)
    for f, k, slab in places:
        right = pair_of_rows(2, slab)
        for parity in range(2):
            from_right = jnp.where(col == COLS - 1, 0.0, pltpu.roll(right[parity], COLS - 1, 0))
            hold(first_frame + f, 2 * k + parity, acc[0, parity, slab] + from_right)


def kernel(
    x_hbm, gain_in_hbm, shift_in_hbm, w1_hbm, gain_mid_hbm, shift_mid_hbm, w2_hbm, short_hbm,
    out_ref,
    xr, xa, hr, ha, w1, s1, w2, s2, short, acc, skip, gain_in, shift_in, gain_mid, shift_mid,
    stat_out, stat_size, stat_in_a, stat_in_b, stat_in_c, stat_in_d,
    load_sem, stat_send, stat_recv, x_send, x_recv, h_send, h_recv,
):
    tm = lax.axis_index("tm")
    z = lax.axis_index("rows")
    last_tm = lax.axis_size("tm") - 1
    last_z = lax.axis_size("rows") - 1
    here = {"y": tm // 8, "x": (tm // 2) % 4, "core": tm % 2, "z": z}

    def partner(axes, offset):
        there = dict(here)
        for a, o in zip(axes, offset):
            there[a] = lax.rem(here[a] + o, SIZES[a])
        return ((there["y"] * 4 + there["x"]) * 2 + there["core"], there["z"])

    barrier = pltpu.get_barrier_semaphore()
    stage_partners = [
        [[partner(axes, o) for o in offsets(axes)] for axes in stages] for stages in STAGES
    ]
    stat_in = ((stat_in_a, stat_in_b), (stat_in_c, stat_in_d))

    loads = [
        pltpu.make_async_copy(src, dst, load_sem.at[i])
        for i, (src, dst) in enumerate(
            [
                (x_hbm.at[0], xr.at[2, 1:9]),
                (gain_in_hbm, gain_in),
                (shift_in_hbm, shift_in),
                (short_hbm, short),
                (w1_hbm, w1),
                (gain_mid_hbm, gain_mid),
                (shift_mid_hbm, shift_mid),
                (w2_hbm, w2),
                (x_hbm.at[1], xr.at[3, 1:9]),
                (x_hbm.at[2], xr.at[4, 1:9]),
                (x_hbm.at[3], xr.at[5, 1:9]),
            ]
        )
    ]
    frame_loads = [loads[0], *loads[8:]]
    for load in frame_loads:
        load.start()

    for target in itertools.chain(*stage_partners[0]):
        pl.semaphore_signal(barrier, inc=1, device_id=target, device_id_type=MESH)

    def greet(ok, target):
        @pl.when(ok)
        def _():
            pl.semaphore_signal(barrier, inc=1, device_id=target, device_id_type=MESH)

    greet(tm > 0, (tm - 1, z))
    greet((tm > 0) & (z > 0), (tm - 1, z - 1))
    greet((tm > 0) & (z < last_z), (tm - 1, z + 1))

    has_next = tm < last_tm
    has_prev = tm > 0
    has_above = z > 0
    has_below = z < last_z

    def halo_copies(src, ext, send, recv, parts):
        frames = {"all": (0, 4), "late": (2, 4), "early": (0, 2)}
        made = []
        for part in parts:
            kind, span, slot = part
            lo, hi = frames[span]
            if kind == "next":
                made.append(
                    (has_next, has_prev, src(2, 4, 0, 8), ext.at[0:2, 1:9], (tm + 1, z), slot)
                )
            elif kind == "down":
                made.append(
                    (has_below, has_above, src(lo, hi, 7, 8), ext.at[2 + lo : 2 + hi, 0:1],
                     (tm, z + 1), slot)
                )
            elif kind == "up":
                made.append(
                    (has_above, has_below, src(lo, hi, 0, 1), ext.at[2 + lo : 2 + hi, 9:10],
                     (tm, z - 1), slot)
                )
            elif kind == "next_down":
                made.append(
                    (has_next & has_below, has_prev & has_above, src(2, 4, 7, 8),
                     ext.at[0:2, 0:1], (tm + 1, z + 1), slot)
                )
            else:
                made.append(
                    (has_next & has_above, has_prev & has_below, src(2, 4, 0, 1),
                     ext.at[0:2, 9:10], (tm + 1, z - 1), slot)
                )
        copies = []
        for sends, gets, source, target, device, slot in made:
            copy = pltpu.make_async_remote_copy(
                src_ref=source, dst_ref=target, send_sem=send.at[slot], recv_sem=recv.at[slot],
                device_id=device, device_id_type=MESH,
            )
            copies.append((sends, gets, copy))
        return copies

    def start(copies):
        for sends, _, copy in copies:
            pl.when(sends)(copy.start)

    def wait_sent(copies):
        for sends, _, copy in copies:
            pl.when(sends)(copy.wait_send)

    def wait_received(copies):
        for _, gets, copy in copies:
            pl.when(gets)(copy.wait_recv)

    def slot_of(buffer, i):
        depth = buffer.shape[1]
        return buffer.at[i // depth, i % depth : i % depth + 1]

    def stat_copies(which, stage):
        return [
            pltpu.make_async_remote_copy(
                src_ref=stat_out.at[which, stage], dst_ref=slot_of(stat_in[which][stage], i),
                send_sem=stat_send.at[which, stage], recv_sem=stat_recv.at[which, stage],
                device_id=target, device_id_type=MESH,
            )
            for i, target in enumerate(stage_partners[which][stage])
        ]

    def wait_for(which, stage, sems):
        size = stat_size.at[0 : len(stage_partners[which][stage])]
        pltpu.make_async_copy(size, size, sems.at[which, stage]).wait()

    def exchange(which, packed, count, meanwhile):
        for stage in range(2):
            buffer = stat_in[which][stage]
            stat_out[which, stage] = packed
            for copy in stat_copies(which, stage):
                copy.start()
            meanwhile(stage)
            if buffer.shape[1] > 1:
                slot_of(buffer, len(stage_partners[which][stage]))[...] = packed
            wait_for(which, stage, stat_recv)
            packed, members = combined(packed, buffer[...], count)
            count = count * members
        return packed, count

    def coefficients(packed, count, channels, gain, shift):
        mean, spread = unpacked(packed, channels)
        inverse = lax.rsqrt(spread * (1.0 / count) + EPSILON)
        return to_lanes(mean), 0.5 * gain[...] * to_lanes(inverse), 0.5 * shift[...]

    def activate_own(raw, out, mean, scale, shift):
        def body(i, carry):
            activate_slab(raw, out, 2 + i // ROWS, 1 + i % ROWS, mean, scale, shift)
            return carry

        lax.fori_loop(0, FRAMES * ROWS, body, 0, unroll=UNROLL)

    def activate_edges(raw, out, lo, hi, mean, scale, shift):
        for row, ok in ((0, has_above), (9, has_below)):

            @pl.when(ok)
            def _():
                for f in range(lo, hi):
                    activate_slab(raw, out, f, row, mean, scale, shift)

            @pl.when(jnp.logical_not(ok))
            def _():
                out[lo:hi, row % 2, row // 2] = jnp.zeros((hi - lo, COLS, out.shape[-1]), BF16)

    def activate_past(raw, out, mean, scale, shift):
        @pl.when(has_prev)
        def _():
            def body(i, carry):
                activate_slab(raw, out, i // ROWS, 1 + i % ROWS, mean, scale, shift)
                return carry

            lax.fori_loop(0, 2 * ROWS, body, 0, unroll=UNROLL)
            activate_edges(raw, out, 0, 2, mean, scale, shift)

        @pl.when(jnp.logical_not(has_prev))
        def _():
            def body(r, carry):
                out[0, r % 2, r // 2] = out[2, r % 2, r // 2]
                out[1, r % 2, r // 2] = out[2, r % 2, r // 2]
                return carry

            lax.fori_loop(0, ROWS + 2, body, 0)

    x_copies = halo_copies(
        lambda f0, f1, r0, r1: x_hbm.at[f0:f1, r0:r1], xr, x_send, x_recv,
        [("down", "all", 0), ("up", "all", 1), ("next", "all", 2),
         ("next_down", "all", 3), ("next_up", "all", 4)],
    )

    def own_hidden(f0, f1, r0, r1):
        return hr.at[2 + f0 : 2 + f1, 1 + r0 : 1 + r1]

    h_late = halo_copies(
        own_hidden, hr, h_send, h_recv,
        [("next", "all", 0), ("next_down", "all", 1), ("next_up", "all", 2),
         ("down", "late", 3), ("up", "late", 4)],
    )
    h_early = halo_copies(
        own_hidden, hr, h_send, h_recv, [("down", "early", 5), ("up", "early", 6)]
    )

    frame_loads[0].wait()
    pivot = group_pivot(xr, 2)
    sums = no_sums(xr.shape[-1])
    for f in range(FRAMES):
        if f > 0:
            frame_loads[f].wait()
        sums = add_up(xr, 2 + f, 1, to_lanes(pivot), sums)
    for load in loads[1:8]:
        load.start()
    packed = packed_statistics(pivot, sums)
    pl.semaphore_wait(
        barrier,
        sum(len(p) for p in stage_partners[0])
        + has_next.astype(jnp.int32)
        + (has_next & has_above).astype(jnp.int32)
        + (has_next & has_below).astype(jnp.int32),
    )

    def during_first(stage):
        if stage == 0:
            loads[3].wait()
            skip[...] = jnp.dot(
                xr[2:6, 1:9].reshape(CELLS, xr.shape[-1]), short[...], preferred_element_type=F32
            )
            loads[7].wait()
            transform_weights(w2, s2)
        if stage == 1:
            start(x_copies)
            loads[4].wait()
            transform_weights(w1, s1)

    packed, count = exchange(0, packed, CELLS * (xr.shape[-1] // GROUPS), during_first)
    loads[1].wait()
    loads[2].wait()
    mean, scale, shift = coefficients(packed, count, xr.shape[-1], gain_in, shift_in)
    activate_own(xr, xa, mean, scale, shift)
    wait_received(x_copies[:2])
    activate_edges(xr, xa, 2, 6, mean, scale, shift)

    def hold_hidden(frame, row, values):
        hr[2 + frame, 1 + row] = values.astype(BF16)

    convolve(xa, w1, s1, acc, hold_hidden, 2, 2)
    start(h_late)
    pivot = group_pivot(hr, 4)
    sums = add_up(hr, 4, 2, to_lanes(pivot), no_sums(hr.shape[-1]))
    wait_received(x_copies[2:])
    activate_past(xr, xa, mean, scale, shift)
    convolve(xa, w1, s1, acc, hold_hidden, 0, 2)

    sums = add_up(hr, 2, 2, to_lanes(pivot), sums)
    packed = packed_statistics(pivot, sums)

    def during_second(stage):
        if stage == 0:
            start(h_early)

    packed, count = exchange(1, packed, CELLS * (hr.shape[-1] // GROUPS), during_second)
    loads[5].wait()
    loads[6].wait()
    mean, scale, shift = coefficients(packed, count, hr.shape[-1], gain_mid, shift_mid)
    activate_own(hr, ha, mean, scale, shift)
    wait_received(h_late)
    wait_received(h_early)
    activate_edges(hr, ha, 2, 6, mean, scale, shift)
    activate_past(hr, ha, mean, scale, shift)

    def hold_decoded(frame, row, values):
        cell = (frame * ROWS + row) * COLS
        out_ref[frame, row] = (values + skip[cell : cell + COLS]).astype(BF16)

    convolve(ha, w2, s2, acc, hold_decoded, 0, 4)

    wait_sent(x_copies)
    wait_sent(h_late)
    wait_sent(h_early)
    for which in range(2):
        for stage in range(2):
            wait_for(which, stage, stat_send)


def per_device(features, gain_in, shift_in, conv_in, gain_mid, shift_mid, conv_out, shortcut):
    c_in = features.shape[-1]
    c_out = shortcut.shape[-1]
    half = (ROWS + 2) // 2
    whole = pl.BlockSpec(memory_space=pl.ANY)
    return pl.pallas_call(
        kernel,
        out_shape=pltpu.VMEM((FRAMES, ROWS, COLS, c_out), BF16),
        in_specs=[whole] * 8,
        out_specs=pl.BlockSpec(memory_space=pltpu.VMEM),
        scratch_shapes=[
            pltpu.VMEM((FRAMES + 2, ROWS + 2, COLS, c_in), BF16),
            pltpu.VMEM((FRAMES + 2, 2, half, COLS, c_in), BF16),
            pltpu.VMEM((FRAMES + 2, ROWS + 2, COLS, c_out), BF16),
            pltpu.VMEM((FRAMES + 2, 2, half, COLS, c_out), BF16),
            pltpu.VMEM(conv_in.shape, BF16),
            pltpu.VMEM((3, 2, 3, c_in, c_out), BF16),
            pltpu.VMEM(conv_out.shape, BF16),
            pltpu.VMEM((3, 2, 3, c_out, c_out), BF16),
            pltpu.VMEM(shortcut.shape, BF16),
            pltpu.VMEM((3, 4, CELLS // 2, c_out), F32),
            pltpu.VMEM((CELLS, c_out), F32),
            pltpu.VMEM((1, c_in), F32),
            pltpu.VMEM((1, c_in), F32),
            pltpu.VMEM((1, c_out), F32),
            pltpu.VMEM((1, c_out), F32),
            pltpu.VMEM((2, 2, 1, 128), F32),
            pltpu.VMEM((127, 1, 128), F32),
            *[pltpu.VMEM((*slots, 128), F32) for slots in ((15, 1), (15, 1), (1, 1), (16, 8))],
            pltpu.SemaphoreType.DMA((11,)),
            pltpu.SemaphoreType.DMA((2, 2)),
            pltpu.SemaphoreType.DMA((2, 2)),
            pltpu.SemaphoreType.DMA((5,)),
            pltpu.SemaphoreType.DMA((5,)),
            pltpu.SemaphoreType.DMA((7,)),
            pltpu.SemaphoreType.DMA((7,)),
        ],
        compiler_params=pltpu.CompilerParams(
            collective_id=0, has_side_effects=True, vmem_limit_bytes=60 * 2**20
        ),
        name="residual_block",
    )(
        features, gain_in.reshape(1, -1), shift_in.reshape(1, -1), conv_in,
        gain_mid.reshape(1, -1), shift_mid.reshape(1, -1), conv_out, shortcut,
    )


def solution(mesh):
    return jax.shard_map(
        per_device,
        mesh=mesh,
        in_specs=(P("tm", "rows", None, None), P(), P(), P(), P(), P(), P(), P()),
        out_specs=P("tm", "rows", None, None),
        check_vma=False,
    )
```

```python
import itertools

import jax
import jax.numpy as jnp
from jax import lax
from jax.experimental import pallas as pl
from jax.experimental.pallas import tpu as pltpu
from jax.sharding import PartitionSpec as P

GROUPS = 32
FRAMES = 4
ROWS = 8
COLS = 32
CELLS = FRAMES * ROWS * COLS
EPSILON = 1e-06
F32 = jnp.float32
BF16 = jnp.bfloat16
MESH = pl.DeviceIdType.MESH
SIZES = {"y": 4, "x": 4, "core": 2, "z": 8}
UNROLL = 8
STAGES = ((("z", "core"), ("y", "x")), (("core",), ("y", "x", "z")))
HOPS = {2: (0, 1), 4: (0, 1, 2, 1), 8: (0, 1, 2, 3, 4, 3, 2, 1)}


def offsets(axes):
    every = itertools.product(*[range(SIZES[a]) for a in axes])
    moved = [o for o in every if any(o)]
    return sorted(moved, key=lambda o: -sum(HOPS[SIZES[a]][i] for a, i in zip(axes, o)))


def group_sum(values, width):
    lane = lax.broadcasted_iota(jnp.int32, values.shape, 1)
    step = 1
    while step < width:
        up = pltpu.roll(values, 128 - step, 1)
        down = pltpu.roll(values, step, 1)
        values = values + jnp.where((lane // step) % 2 == 0, up, down)
        step *= 2
    return values


def to_rows(values):
    return jnp.concatenate([values[:, i : i + 128] for i in range(0, values.shape[1], 128)], axis=0)


def to_lanes(values):
    return jnp.concatenate([values[i : i + 1, :] for i in range(values.shape[0])], axis=1)


def group_pivot(ext, frame):
    channels = ext.shape[-1]
    width = channels // GROUPS
    cell = to_rows(ext[frame, 1].astype(F32)[0:1])
    lane = lax.broadcasted_iota(jnp.int32, cell.shape, 1)
    return group_sum(jnp.where(lane % width == 0, cell, 0.0), width)


def add_up(ext, first, frames, pivot, sums):
    channels = ext.shape[-1]
    slabs = 4

    def body(i, carry):
        total, spread = carry
        for j in range(slabs):
            n = i * slabs + j
            moved = ext[first + n // ROWS, 1 + n % ROWS].astype(F32) - pivot
            parts = moved.reshape(COLS // 8, 8, channels)
            total = total + parts.sum(0)
            spread = spread + jnp.square(parts).sum(0)
        return total, spread

    return lax.fori_loop(0, frames * ROWS // slabs, body, sums)


def no_sums(channels):
    return jnp.zeros((8, channels), F32), jnp.zeros((8, channels), F32)


def packed_statistics(pivot, sums):
    total, spread = sums
    channels = total.shape[-1]
    width = channels // GROUPS
    rows = channels // 128
    both = jnp.concatenate(
        [to_rows(total.sum(0, keepdims=True)), to_rows(spread.sum(0, keepdims=True))], axis=0
    )
    both = group_sum(both, width)
    offset = both[:rows] * (1.0 / (CELLS * width))
    mean = pivot + offset
    spread = both[rows:] - both[:rows] * offset
    lane = lax.broadcasted_iota(jnp.int32, (1, 128), 1)
    packed = jnp.zeros((1, 128), F32)
    for r in range(rows):
        pair = jnp.where(lane % 4 < 2, mean[r : r + 1], spread[r : r + 1])
        packed = packed + jnp.where((lane % width) // 4 == r, pair, 0.0)
    return packed


def combined(own, others, count):
    held = others.shape[0] * others.shape[1]
    full = held % 2 == 0
    members = held if full else held + 1
    lane = lax.broadcasted_iota(jnp.int32, (1, 128), 1)

    def over_all(values):
        return jnp.sum(jnp.sum(values, axis=0), axis=0, keepdims=True)

    total = over_all(others) if full else own + over_all(others)
    mean = total * (1.0 / members)
    deviation = over_all(jnp.square(others - mean[None]))
    if not full:
        deviation = deviation + jnp.square(own - mean)
    moved = pltpu.roll(deviation, 2, 1)
    return jnp.where(lane % 4 < 2, mean, total + moved * float(count)), members


def unpacked(packed, channels):
    width = channels // GROUPS
    rows = channels // 128
    shape = (2 * rows, 128)
    lane = lax.broadcasted_iota(jnp.int32, shape, 1)
    row = lax.broadcasted_iota(jnp.int32, shape, 0)
    wanted = jnp.where(row < rows, 4 * row, 4 * (row - rows) + 2)
    picked = jnp.where(lane % width == wanted, jnp.broadcast_to(packed, shape), 0.0)
    spread = group_sum(picked, width)
    return spread[:rows], spread[rows:]


def activate_slab(raw, out, frame, row, mean, scale, shift):
    v = (raw[frame, row].astype(F32) - mean) * scale + shift
    out[frame, row % 2, row // 2] = (v + v * jnp.tanh(v)).astype(BF16)


def transform_weights(weights, sums):
    depth = weights.shape[3]
    step = 64

    def body(i, carry):
        tap, part = i // (depth // step), i % (depth // step)
        a, e = tap // 3, tap % 3
        k = pl.ds(pl.multiple_of(part * step, step), step)
        outer = 0.5 * (weights[a, 0, e, k].astype(F32) + weights[a, 2, e, k].astype(F32))
        middle = 0.5 * weights[a, 1, e, k].astype(F32)
        sums[a, 0, e, k] = (outer + middle).astype(BF16)
        sums[a, 1, e, k] = (outer - middle).astype(BF16)
        return carry

    lax.fori_loop(0, 9 * (depth // step), body, 0)


def convolve(act, weights, sums, acc, hold, first_frame, frames):
    channels = act.shape[-1]
    width = weights.shape[-1]
    half = ROWS // 2
    cells = frames * half * COLS
    col = lax.broadcasted_iota(jnp.int32, (COLS, width), 0)

    def rows(a, parity, k):
        frame = first_frame + a
        return act[frame : frame + frames, parity, k : k + half].reshape(cells, channels)

    inputs = [
        lambda a: rows(a, 0, 0) - rows(a, 0, 1),
        lambda a: rows(a, 1, 0) + rows(a, 0, 1),
        lambda a: rows(a, 0, 1) - rows(a, 1, 0),
        lambda a: rows(a, 1, 0) - rows(a, 1, 1),
    ]

    def one_column_tap(e):
        matrices = [weights[:, 0, e], sums[:, 0, e], sums[:, 1, e], weights[:, 2, e]]
        for i in range(4):
            taps = jnp.concatenate([inputs[i](a) for a in range(3)], axis=-1)
            acc[e, i, 0:cells] = jnp.dot(
                taps, matrices[i].reshape(3 * channels, width), preferred_element_type=F32
            )

    def pair_of_rows(e, slab):
        m = [acc[e, i, slab] for i in range(4)]
        return m[0] + (m[1] + m[2]), (m[1] - m[2]) - m[3]

    places = [
        (f, k, slice((f * half + k) * COLS, (f * half + k + 1) * COLS))
        for f in range(frames)
        for k in range(half)
    ]
    one_column_tap(0)
    one_column_tap(1)
    for _, _, slab in places:
        left, middle = pair_of_rows(0, slab), pair_of_rows(1, slab)
        for parity in range(2):
            from_left = jnp.where(col == 0, 0.0, pltpu.roll(left[parity], 1, 0))
            acc[0, parity, slab] = middle[parity] + from_left
    one_column_tap(2)
    for f, k, slab in places:
        right = pair_of_rows(2, slab)
        for parity in range(2):
            from_right = jnp.where(col == COLS - 1, 0.0, pltpu.roll(right[parity], COLS - 1, 0))
            hold(first_frame + f, 2 * k + parity, acc[0, parity, slab] + from_right)


def kernel(
    x_hbm, gain_in_hbm, shift_in_hbm, w1_hbm, gain_mid_hbm, shift_mid_hbm, w2_hbm, short_hbm,
    out_ref,
    xr, xa, hr, ha, w1, s1, w2, s2, short, acc, skip, gain_in, shift_in, gain_mid, shift_mid,
    stat_out, stat_size, stat_in_a, stat_in_b, stat_in_c, stat_in_d,
    load_sem, stat_send, stat_recv, x_send, x_recv, h_send, h_recv,
):
    tm = lax.axis_index("tm")
    z = lax.axis_index("rows")
    last_tm = lax.axis_size("tm") - 1
    last_z = lax.axis_size("rows") - 1
    here = {"y": tm // 8, "x": (tm // 2) % 4, "core": tm % 2, "z": z}

    def partner(axes, offset):
        there = dict(here)
        for a, o in zip(axes, offset):
            there[a] = lax.rem(here[a] + o, SIZES[a])
        return ((there["y"] * 4 + there["x"]) * 2 + there["core"], there["z"])

    barrier = pltpu.get_barrier_semaphore()
    stage_partners = [
        [[partner(axes, o) for o in offsets(axes)] for axes in stages] for stages in STAGES
    ]
    stat_in = ((stat_in_a, stat_in_b), (stat_in_c, stat_in_d))

    loads = [
        pltpu.make_async_copy(src, dst, load_sem.at[i])
        for i, (src, dst) in enumerate(
            [
                (x_hbm.at[0], xr.at[2, 1:9]),
                (gain_in_hbm, gain_in),
                (shift_in_hbm, shift_in),
                (short_hbm, short),
                (w1_hbm, w1),
                (gain_mid_hbm, gain_mid),
                (shift_mid_hbm, shift_mid),
                (w2_hbm, w2),
                (x_hbm.at[1], xr.at[3, 1:9]),
                (x_hbm.at[2], xr.at[4, 1:9]),
                (x_hbm.at[3], xr.at[5, 1:9]),
            ]
        )
    ]
    frame_loads = [loads[0], *loads[8:]]
    for load in frame_loads:
        load.start()

    for target in itertools.chain(*stage_partners[0]):
        pl.semaphore_signal(barrier, inc=1, device_id=target, device_id_type=MESH)

    def greet(ok, target):
        @pl.when(ok)
        def _():
            pl.semaphore_signal(barrier, inc=1, device_id=target, device_id_type=MESH)

    greet(tm > 0, (tm - 1, z))
    greet((tm > 0) & (z > 0), (tm - 1, z - 1))
    greet((tm > 0) & (z < last_z), (tm - 1, z + 1))

    has_next = tm < last_tm
    has_prev = tm > 0
    has_above = z > 0
    has_below = z < last_z

    def halo_copies(src, ext, send, recv, parts):
        frames = {"all": (0, 4), "late": (2, 4), "early": (0, 2)}
        made = []
        for part in parts:
            kind, span, slot = part
            lo, hi = frames[span]
            if kind == "next":
                made.append(
                    (has_next, has_prev, src(2, 4, 0, 8), ext.at[0:2, 1:9], (tm + 1, z), slot)
                )
            elif kind == "down":
                made.append(
                    (has_below, has_above, src(lo, hi, 7, 8), ext.at[2 + lo : 2 + hi, 0:1],
                     (tm, z + 1), slot)
                )
            elif kind == "up":
                made.append(
                    (has_above, has_below, src(lo, hi, 0, 1), ext.at[2 + lo : 2 + hi, 9:10],
                     (tm, z - 1), slot)
                )
            elif kind == "next_down":
                made.append(
                    (has_next & has_below, has_prev & has_above, src(2, 4, 7, 8),
                     ext.at[0:2, 0:1], (tm + 1, z + 1), slot)
                )
            else:
                made.append(
                    (has_next & has_above, has_prev & has_below, src(2, 4, 0, 1),
                     ext.at[0:2, 9:10], (tm + 1, z - 1), slot)
                )
        copies = []
        for sends, gets, source, target, device, slot in made:
            copy = pltpu.make_async_remote_copy(
                src_ref=source, dst_ref=target, send_sem=send.at[slot], recv_sem=recv.at[slot],
                device_id=device, device_id_type=MESH,
            )
            copies.append((sends, gets, copy))
        return copies

    def start(copies):
        for sends, _, copy in copies:
            pl.when(sends)(copy.start)

    def wait_sent(copies):
        for sends, _, copy in copies:
            pl.when(sends)(copy.wait_send)

    def wait_received(copies):
        for _, gets, copy in copies:
            pl.when(gets)(copy.wait_recv)

    def slot_of(buffer, i):
        depth = buffer.shape[1]
        return buffer.at[i // depth, i % depth : i % depth + 1]

    def stat_copies(which, stage):
        return [
            pltpu.make_async_remote_copy(
                src_ref=stat_out.at[which, stage], dst_ref=slot_of(stat_in[which][stage], i),
                send_sem=stat_send.at[which, stage], recv_sem=stat_recv.at[which, stage],
                device_id=target, device_id_type=MESH,
            )
            for i, target in enumerate(stage_partners[which][stage])
        ]

    def wait_for(which, stage, sems):
        size = stat_size.at[0 : len(stage_partners[which][stage])]
        pltpu.make_async_copy(size, size, sems.at[which, stage]).wait()

    def exchange(which, packed, count, meanwhile):
        for stage in range(2):
            buffer = stat_in[which][stage]
            stat_out[which, stage] = packed
            for copy in stat_copies(which, stage):
                copy.start()
            meanwhile(stage)
            if buffer.shape[1] > 1:
                slot_of(buffer, len(stage_partners[which][stage]))[...] = packed
            wait_for(which, stage, stat_recv)
            packed, members = combined(packed, buffer[...], count)
            count = count * members
        return packed, count

    def coefficients(packed, count, channels, gain, shift):
        mean, spread = unpacked(packed, channels)
        inverse = lax.rsqrt(spread * (1.0 / count) + EPSILON)
        return to_lanes(mean), 0.5 * gain[...] * to_lanes(inverse), 0.5 * shift[...]

    def activate_own(raw, out, mean, scale, shift):
        def body(i, carry):
            activate_slab(raw, out, 2 + i // ROWS, 1 + i % ROWS, mean, scale, shift)
            return carry

        lax.fori_loop(0, FRAMES * ROWS, body, 0, unroll=UNROLL)

    def activate_edges(raw, out, lo, hi, mean, scale, shift):
        for row, ok in ((0, has_above), (9, has_below)):

            @pl.when(ok)
            def _():
                for f in range(lo, hi):
                    activate_slab(raw, out, f, row, mean, scale, shift)

            @pl.when(jnp.logical_not(ok))
            def _():
                out[lo:hi, row % 2, row // 2] = jnp.zeros((hi - lo, COLS, out.shape[-1]), BF16)

    def activate_past(raw, out, mean, scale, shift):
        @pl.when(has_prev)
        def _():
            def body(i, carry):
                activate_slab(raw, out, i // ROWS, 1 + i % ROWS, mean, scale, shift)
                return carry

            lax.fori_loop(0, 2 * ROWS, body, 0, unroll=UNROLL)
            activate_edges(raw, out, 0, 2, mean, scale, shift)

        @pl.when(jnp.logical_not(has_prev))
        def _():
            def body(r, carry):
                out[0, r % 2, r // 2] = out[2, r % 2, r // 2]
                out[1, r % 2, r // 2] = out[2, r % 2, r // 2]
                return carry

            lax.fori_loop(0, ROWS + 2, body, 0)

    x_copies = halo_copies(
        lambda f0, f1, r0, r1: x_hbm.at[f0:f1, r0:r1], xr, x_send, x_recv,
        [("down", "all", 0), ("up", "all", 1), ("next", "all", 2),
         ("next_down", "all", 3), ("next_up", "all", 4)],
    )

    def own_hidden(f0, f1, r0, r1):
        return hr.at[2 + f0 : 2 + f1, 1 + r0 : 1 + r1]

    h_late = halo_copies(
        own_hidden, hr, h_send, h_recv,
        [("next", "all", 0), ("next_down", "all", 1), ("next_up", "all", 2),
         ("down", "late", 3), ("up", "late", 4)],
    )
    h_early = halo_copies(
        own_hidden, hr, h_send, h_recv, [("down", "early", 5), ("up", "early", 6)]
    )

    frame_loads[0].wait()
    pivot = group_pivot(xr, 2)
    sums = no_sums(xr.shape[-1])
    for f in range(FRAMES):
        if f > 0:
            frame_loads[f].wait()
        sums = add_up(xr, 2 + f, 1, to_lanes(pivot), sums)
    for load in loads[1:8]:
        load.start()
    packed = packed_statistics(pivot, sums)
    pl.semaphore_wait(
        barrier,
        sum(len(p) for p in stage_partners[0])
        + has_next.astype(jnp.int32)
        + (has_next & has_above).astype(jnp.int32)
        + (has_next & has_below).astype(jnp.int32),
    )

    def during_first(stage):
        if stage == 0:
            loads[3].wait()
            skip[...] = jnp.dot(
                xr[2:6, 1:9].reshape(CELLS, xr.shape[-1]), short[...], preferred_element_type=F32
            )
            loads[7].wait()
            transform_weights(w2, s2)
        if stage == 1:
            start(x_copies)
            loads[4].wait()
            transform_weights(w1, s1)

    packed, count = exchange(0, packed, CELLS * (xr.shape[-1] // GROUPS), during_first)
    loads[1].wait()
    loads[2].wait()
    mean, scale, shift = coefficients(packed, count, xr.shape[-1], gain_in, shift_in)
    activate_own(xr, xa, mean, scale, shift)
    wait_received(x_copies[:2])
    activate_edges(xr, xa, 2, 6, mean, scale, shift)

    def hold_hidden(frame, row, values):
        hr[2 + frame, 1 + row] = values.astype(BF16)

    convolve(xa, w1, s1, acc, hold_hidden, 2, 2)
    pivot = group_pivot(hr, 4)
    sums = add_up(hr, 4, 2, to_lanes(pivot), no_sums(hr.shape[-1]))
    wait_received(x_copies[2:])
    activate_past(xr, xa, mean, scale, shift)
    convolve(xa, w1, s1, acc, hold_hidden, 0, 2)

    sums = add_up(hr, 2, 2, to_lanes(pivot), sums)
    packed = packed_statistics(pivot, sums)

    def during_second(stage):
        if stage == 1:
            start(h_late)
            start(h_early)

    packed, count = exchange(1, packed, CELLS * (hr.shape[-1] // GROUPS), during_second)
    loads[5].wait()
    loads[6].wait()
    mean, scale, shift = coefficients(packed, count, hr.shape[-1], gain_mid, shift_mid)
    activate_own(hr, ha, mean, scale, shift)
    wait_received(h_late)
    wait_received(h_early)
    activate_edges(hr, ha, 2, 6, mean, scale, shift)
    activate_past(hr, ha, mean, scale, shift)

    def hold_decoded(frame, row, values):
        cell = (frame * ROWS + row) * COLS
        out_ref[frame, row] = (values + skip[cell : cell + COLS]).astype(BF16)

    convolve(ha, w2, s2, acc, hold_decoded, 0, 4)

    wait_sent(x_copies)
    wait_sent(h_late)
    wait_sent(h_early)
    for which in range(2):
        for stage in range(2):
            wait_for(which, stage, stat_send)


def per_device(features, gain_in, shift_in, conv_in, gain_mid, shift_mid, conv_out, shortcut):
    c_in = features.shape[-1]
    c_out = shortcut.shape[-1]
    half = (ROWS + 2) // 2
    whole = pl.BlockSpec(memory_space=pl.ANY)
    return pl.pallas_call(
        kernel,
        out_shape=pltpu.VMEM((FRAMES, ROWS, COLS, c_out), BF16),
        in_specs=[whole] * 8,
        out_specs=pl.BlockSpec(memory_space=pltpu.VMEM),
        scratch_shapes=[
            pltpu.VMEM((FRAMES + 2, ROWS + 2, COLS, c_in), BF16),
            pltpu.VMEM((FRAMES + 2, 2, half, COLS, c_in), BF16),
            pltpu.VMEM((FRAMES + 2, ROWS + 2, COLS, c_out), BF16),
            pltpu.VMEM((FRAMES + 2, 2, half, COLS, c_out), BF16),
            pltpu.VMEM(conv_in.shape, BF16),
            pltpu.VMEM((3, 2, 3, c_in, c_out), BF16),
            pltpu.VMEM(conv_out.shape, BF16),
            pltpu.VMEM((3, 2, 3, c_out, c_out), BF16),
            pltpu.VMEM(shortcut.shape, BF16),
            pltpu.VMEM((3, 4, CELLS // 2, c_out), F32),
            pltpu.VMEM((CELLS, c_out), F32),
            pltpu.VMEM((1, c_in), F32),
            pltpu.VMEM((1, c_in), F32),
            pltpu.VMEM((1, c_out), F32),
            pltpu.VMEM((1, c_out), F32),
            pltpu.VMEM((2, 2, 1, 128), F32),
            pltpu.VMEM((127, 1, 128), F32),
            *[pltpu.VMEM((*slots, 128), F32) for slots in ((15, 1), (15, 1), (1, 1), (16, 8))],
            pltpu.SemaphoreType.DMA((11,)),
            pltpu.SemaphoreType.DMA((2, 2)),
            pltpu.SemaphoreType.DMA((2, 2)),
            pltpu.SemaphoreType.DMA((5,)),
            pltpu.SemaphoreType.DMA((5,)),
            pltpu.SemaphoreType.DMA((7,)),
            pltpu.SemaphoreType.DMA((7,)),
        ],
        compiler_params=pltpu.CompilerParams(
            collective_id=0, has_side_effects=True, vmem_limit_bytes=60 * 2**20
        ),
        name="residual_block",
    )(
        features, gain_in.reshape(1, -1), shift_in.reshape(1, -1), conv_in,
        gain_mid.reshape(1, -1), shift_mid.reshape(1, -1), conv_out, shortcut,
    )


def solution(mesh):
    return jax.shard_map(
        per_device,
        mesh=mesh,
        in_specs=(P("tm", "rows", None, None), P(), P(), P(), P(), P(), P(), P()),
        out_specs=P("tm", "rows", None, None),
        check_vma=False,
    )
```
